32 devices in a mesh: groups: 2 (over x), expert: 16 (over z, y, core).
Axes of the slice: x: 2, y: 2, z: 4, core: 2. Of those that a mesh axis runs over, the one named last changes fastest.
Arguments:
- tokens: bfloat16 [256, 7168], P(('groups', 'expert')), parts along dimension 0, may hold values from -6 to 6
- routes: int32 [256, 8], P(('groups', 'expert')), parts along dimension 0, may hold values from 0 to 15, all different within a row; in each aligned block of 8 rows (0 to 7, 8 to 15, ...) at most 6 rows name the same one
- gate_scale: float32 [256, 8], P(('groups', 'expert')), parts along dimension 0, may hold values from 0.05 to 0.4
- w_gate: bfloat16 [16, 7168, 2048], P('expert'), may hold values from -0.0625 to 0.0625
- w_up: bfloat16 [16, 7168, 2048], P('expert'), may hold values from -0.0625 to 0.0625
- w_down: bfloat16 [16, 2048, 7168], P('expert'), may hold values from -0.125 to 0.125
Outputs:
- mixed: bfloat16 [256, 7168], P(('groups', 'expert')), parts along dimension 0
The draws below stay inside these ranges and needn't reach their ends.
There are 2 independent parts, one for each index of `groups`. The reference program is written for one: setup_inputs(seed, part) draws one part's arguments, and reference() takes and returns one part's arrays. A program takes and returns all parts, laid end to end along the dimension named above; an argument that names none is the same for every part. Nothing has to cross between parts.
Inputs may be any that keep to these rules, and one draw needn't show every extreme that they name: `routes`: each token names 8 different experts. Among the tokens of one device no expert is named by more than 6 tokens, a bound that some block reaches.
All inputs are finite; a program needn't handle non-finite values.
Results may differ from the reference program's by a relative error of at most 0.0085.
Values may be sent and summed in bfloat16 or wider, within the bound.
A program may use at most 192 MiB of HBM per device.

```python
import math
import jax
import jax.numpy as jnp
import numpy as np
from jax import lax

D = 7168
FF = 2048
TOP = 8
TOK_DEV = 8
EXPERTS = 16
SLICES = 1
FF_DEV = 2048
CAP = 6
TOKENS = 128
N_EXPERT = 16


def steps_of(stream_key, shape, cuts, smallest, top_value):
    def one(dim, shards_of):
        steps = jax.random.uniform(jax.random.fold_in(jax.random.fold_in(stream_key, 6), dim), (shards_of,), jnp.float32, smallest / len(cuts), top_value / len(cuts))
        return jnp.repeat(jnp.exp(steps), shape[dim] // shards_of).reshape((-1,) + (1,) * (len(shape) - dim - 1))

    level = one(*cuts[0])
    for cut in cuts[1:]:
        level = level * one(*cut)
    return level


def shared_out(rng, own, number, rows, amount, top, most, slope):
    sequence = jax.random.permutation(rng, amount)
    crowded, usual = load_shares(amount, rows * top, most, slope, True), load_shares(amount, rows * top, most, slope, False)
    places = jnp.arange(amount)

    def named(lengths, offset_by):
        used = int((lengths > 0).sum())
        fixed = max(1, used // 4)
        moved = fixed + (places - fixed + offset_by * (used - fixed)) % max(1, amount - fixed)
        return jnp.zeros((amount,), jnp.int32).at[sequence[jnp.where(places < fixed, places, moved)]].set(jnp.asarray(lengths, jnp.int32))

    lengths = jnp.where(number % 4 == 0, named(crowded, number // 4), named(usual, number - number // 4 - 1))
    mixed = jax.random.permutation(jax.random.fold_in(own, 3), amount)
    giver, taker = mixed[0:amount // 2 * 2:2], mixed[1:amount // 2 * 2:2]
    slack = jnp.minimum(lengths[giver] - 1, most - lengths[taker]) // 2
    slack = jnp.where((giver == sequence[0]) | (taker == sequence[0]) | (lengths[taker] == 0), 0, jnp.maximum(slack, 0))
    moved = jax.random.randint(jax.random.fold_in(own, 4), (amount // 2,), 0, 1 << 20) % (slack + 1)
    lengths = lengths.at[giver].add(-moved).at[taker].add(moved)
    members = jnp.searchsorted(jnp.cumsum(lengths), jnp.arange(rows * top), side="right").astype(jnp.int32)
    grid = members.reshape(top, rows).T
    grid = grid[jax.random.permutation(jax.random.fold_in(own, 1), rows)]
    offset_by = jax.random.randint(jax.random.fold_in(own, 2), (rows, 1), 0, top)
    return jnp.take_along_axis(grid, (jnp.arange(top)[None, :] + offset_by) % top, axis=1)


def load_shares(amount, total, reach, slope, full):
    loads = [(1 << 20) // math.isqrt(grade ** slope) + 1 for grade in range(1, amount + 1)]
    largest = reach if full else min(reach, max(-(-total // amount), total * loads[0] // sum(loads)))
    least = 1 if total - largest >= amount - 1 else 0
    counts, spare = [largest] + [least] * (amount - 1), total - largest - least * (amount - 1)
    while spare > 0:
        movable = [i for i in range(1, amount) if counts[i] < largest] or [i for i in range(1, amount) if counts[i] < reach]
        mass, left = sum([loads[i] for i in movable]), spare
        for i in movable:
            addition = min(reach - counts[i], max(1, left * loads[i] // mass), spare)
            counts[i] = counts[i] + addition
            spare = spare - addition
    return np.array(counts)


def noise(rng, shape, deviation, limit, shards=(), kind=jnp.bfloat16):
    array = deviation * jax.random.normal(rng, shape, jnp.float32)
    if shards:
        array = array * steps_of(rng, shape, shards, -0.22, 0.18)
    return jnp.clip(array, -limit, limit).astype(kind)


def setup_inputs(seed: int = 0, part: int = 0) -> dict:
    key_list = jax.random.split(jax.random.key(seed), 7)
    own_keys = jax.random.split(jax.random.fold_in(key_list[6], part), 7)
    tokens = noise(own_keys[0], (TOKENS, D), 1.0, 6.0, ((0, 16),))
    routes_keys = jax.random.split(jax.random.fold_in(own_keys[1], 1), TOKENS // TOK_DEV)
    routes_turns = jax.random.permutation(jax.random.fold_in(own_keys[1], 3), TOKENS // TOK_DEV)
    routes = jax.vmap(lambda own, number: shared_out(jax.random.fold_in(own_keys[1], 2), own, number, TOK_DEV, EXPERTS, TOP, CAP, 2))(routes_keys, routes_turns).reshape((TOKENS, TOP))
    gate_scale = jnp.clip(0.05 + 0.35 * jax.random.uniform(own_keys[2], (TOKENS, TOP), jnp.float32) ** steps_of(own_keys[2], (TOKENS, TOP), ((0, 16),), -0.2, 0.2), 0.05, 0.4)
    w_gate = noise(key_list[3], (N_EXPERT, D, FF_DEV), D ** -0.5, 0.0625, ((0, 16),))
    w_up = noise(key_list[4], (N_EXPERT, D, FF_DEV), D ** -0.5, 0.0625, ((0, 16),))
    w_down = noise(key_list[5], (N_EXPERT, FF_DEV, D), FF ** -0.5, 0.125, ((0, 16),))
    return dict(tokens=tokens, routes=routes, gate_scale=gate_scale, w_gate=w_gate, w_up=w_up, w_down=w_down)


def reference(tokens, routes, gate_scale, w_gate, w_up, w_down):
    flat = routes.reshape(N_EXPERT, TOK_DEV * TOP)
    onehot = (flat[:, :, None] == jnp.arange(EXPERTS, dtype=jnp.int32)[None, None, :]).astype(jnp.int32)
    slot = jnp.sum((jnp.cumsum(onehot, axis=1) - onehot) * onehot, axis=2).astype(jnp.int32)
    position = (flat * CAP + slot).astype(jnp.int32)
    tok_of = (jnp.arange(TOK_DEV * TOP, dtype=jnp.int32) // TOP).astype(jnp.int32)
    block_ids = jnp.arange(N_EXPERT, dtype=jnp.int32)[:, None]
    table = jnp.zeros((N_EXPERT, EXPERTS * CAP), jnp.int32)
    table = table.at[block_ids, position].set(jnp.broadcast_to(tok_of + 1, position.shape).astype(jnp.int32))
    blocks = tokens.reshape(N_EXPERT, TOK_DEV, D)
    scales = gate_scale.reshape(N_EXPERT, TOK_DEV * TOP)
    slot_hot = (slot[:, :, None] == jnp.arange(CAP, dtype=jnp.int32)[None, None, :]).astype(jnp.float32)

    def per_expert(total, expert_id):
        index = lax.dynamic_slice_in_dim(table, (expert_id * CAP).astype(jnp.int32), CAP, 1)
        picked = blocks[block_ids, jnp.maximum(index - 1, 0)]
        rows = jnp.where(index[:, :, None] > 0, picked, jnp.zeros_like(picked)).reshape(N_EXPERT * CAP, D)
        summed = jnp.zeros((N_EXPERT * CAP, D), jnp.float32)
        for part in range(SLICES):
            owner = (expert_id * SLICES + part).astype(jnp.int32)
            gate_w = lax.dynamic_index_in_dim(w_gate, owner, 0, keepdims=False)
            up_w = lax.dynamic_index_in_dim(w_up, owner, 0, keepdims=False)
            down_w = lax.dynamic_index_in_dim(w_down, owner, 0, keepdims=False)
            gate = jnp.dot(rows, gate_w, preferred_element_type=jnp.float32)
            upper = jnp.dot(rows, up_w, preferred_element_type=jnp.float32)
            hidden = (jax.nn.silu(gate) * upper).astype(jnp.bfloat16)
            partial_out = jnp.dot(hidden, down_w, preferred_element_type=jnp.float32).astype(jnp.bfloat16)
            summed = summed + partial_out.astype(jnp.float32)
        chosen = (flat == expert_id).astype(jnp.float32) * scales
        weights = (chosen[:, :, None] * slot_hot).reshape(N_EXPERT, TOK_DEV, TOP, CAP).sum(axis=2)
        total = total + jnp.einsum("ntc,ncd->ntd", weights.astype(jnp.float32), summed.reshape(N_EXPERT, CAP, D), precision=lax.Precision.HIGHEST)
        return total, None

    start = jnp.zeros((N_EXPERT, TOK_DEV, D), jnp.float32)
    total, unused = lax.scan(per_expert, start, jnp.arange(EXPERTS, dtype=jnp.int32))
    return total.reshape(TOKENS, D).astype(jnp.bfloat16)
```

```python
import functools
import math

import jax
import jax.numpy as jnp
from jax import lax
from jax.experimental import pallas as pl
from jax.experimental.pallas import tpu as pltpu
from jax.sharding import PartitionSpec as P

FF = 2048
CHUNK = 512
RING = 22
PARTS = 2
LAG = 1
VMEM = 62 * 2**20


def by_all_to_all(tokens, routes, gate_scale, w_gate, w_up, w_down):
    devices = lax.axis_size("expert")
    tok_count, top_count = routes.shape
    width = tokens.shape[1]
    slices = FF // w_gate.shape[2]
    experts = devices // slices
    capacity = tok_count * top_count // experts + 2
    flat = routes.reshape(-1)
    onehot = (flat[:, None] == jnp.arange(experts, dtype=jnp.int32)[None, :]).astype(jnp.int32)
    slot = jnp.sum((jnp.cumsum(onehot, axis=0) - onehot) * onehot, axis=1)
    position = flat * capacity + slot
    picks = position[:, None] == jnp.arange(experts * capacity, dtype=jnp.int32)[None, :]
    picks = picks.reshape(tok_count, top_count, experts * capacity)
    select = jnp.any(picks, axis=1).astype(jnp.bfloat16)
    buffer = lax.dot_general(
        select, tokens, (((0,), (0,)), ((), ())), preferred_element_type=jnp.float32
    ).astype(jnp.bfloat16)
    outgoing = jnp.broadcast_to(
        buffer.reshape(experts, 1, capacity, width), (experts, slices, capacity, width)
    )
    outgoing = outgoing.reshape(devices, capacity, width)
    arrived = lax.all_to_all(outgoing, "expert", split_axis=0, concat_axis=0, tiled=True)
    count = arrived.shape[1]
    flat_rows = arrived.reshape(-1, width)
    gate = jnp.dot(flat_rows, w_gate[0], preferred_element_type=jnp.float32)
    upper = jnp.dot(flat_rows, w_up[0], preferred_element_type=jnp.float32)
    hidden = (jax.nn.silu(gate) * upper).astype(jnp.bfloat16)
    result = jnp.dot(hidden, w_down[0], preferred_element_type=jnp.float32).astype(jnp.bfloat16)
    back = lax.all_to_all(
        result.reshape(devices, count, width), "expert", split_axis=0, concat_axis=0, tiled=True
    )
    summed = back.reshape(experts, slices, capacity, width).astype(jnp.float32).sum(axis=1)
    summed = summed.reshape(experts * capacity, width)
    weights = jnp.sum(picks.astype(jnp.float32) * gate_scale[:, :, None], axis=1)
    mixed = jnp.dot(
        weights, summed, precision=lax.Precision.HIGHEST, preferred_element_type=jnp.float32
    )
    return mixed.astype(jnp.bfloat16)


def kernel(
    bits, slices, tok, routes, gates, wg, wu, wd, out,
    x3, x2, s3, acc_g, acc_u, hid, ring, keep, snd, rcv,
    ring_sem, ag_send, ag_recv, sc_send, sc_recv, rs_send, rs_recv,
):
    steps = len(bits)
    block, width = tok.shape
    rows = block << steps
    hidden = wg.shape[2]
    k_count = width // CHUNK
    part = width // PARTS
    me = lax.axis_index("expert")

    def partner(step):
        place = 1 << bits[step]
        return {"expert": me + (1 - 2 * ((me // place) % 2)) * place}

    def load_pair(p):
        for j, w in enumerate((wg, wu)):
            slot = lax.rem(2 * p + j, RING)
            pltpu.make_async_copy(
                w.at[0, pl.ds(p * CHUNK, CHUNK), :], ring.at[slot], ring_sem.at[slot]
            ).start()

    def load_down(d):
        slot = lax.rem(2 * k_count + d, RING)
        for k in range(hidden // CHUNK):
            pltpu.make_async_copy(
                wd.at[0, pl.ds(k * CHUNK, CHUNK), pl.ds(d * CHUNK, CHUNK)],
                ring.at[slot, :, pl.ds(k * CHUNK, CHUNK)],
                ring_sem.at[slot],
            ).start()

    def arrived(slot):
        pltpu.make_async_copy(ring.at[slot], ring.at[slot], ring_sem.at[slot]).wait()

    def first(p, carry):
        load_pair(p)
        return carry

    lax.fori_loop(0, RING // 2, first, 0)

    barrier = pltpu.get_barrier_semaphore()
    for step in range(steps):
        pl.semaphore_signal(
            barrier, inc=1, device_id=partner(step), device_id_type=pl.DeviceIdType.MESH
        )
    x3[0] = tok[...]
    lane = lax.broadcasted_iota(jnp.int32, (block, 128), 1)
    dense = jnp.zeros((block, 128), jnp.float32)
    for k in range(routes.shape[1]):
        dense += jnp.where(routes[:, k : k + 1] == lane, gates[:, k : k + 1], 0.0)
    s3[0] = dense
    pl.semaphore_wait(barrier, steps)

    def gather(step, a):
        held = 1 << step
        columns = pl.ds(a * part, part)
        return pltpu.make_async_remote_copy(
            src_ref=x3.at[pl.ds(0, held), :, columns],
            dst_ref=x3.at[pl.ds(held, held), :, columns],
            send_sem=ag_send.at[step, a],
            recv_sem=ag_recv.at[step, a],
            device_id=partner(step),
            device_id_type=pl.DeviceIdType.MESH,
        )

    def gather_scale(step):
        held = 1 << step
        return pltpu.make_async_remote_copy(
            src_ref=s3.at[pl.ds(0, held)],
            dst_ref=s3.at[pl.ds(held, held)],
            send_sem=sc_send.at[step],
            recv_sem=sc_recv.at[step],
            device_id=partner(step),
            device_id_type=pl.DeviceIdType.MESH,
        )

    for phase in range(PARTS + steps):
        for a in range(PARTS):
            step = phase - a
            if 0 <= step - 1 < steps:
                gather(step - 1, a).wait_recv()
            if 0 <= step < steps:
                gather(step, a).start()
        if phase < steps + 1:
            if phase > 0:
                gather_scale(phase - 1).wait_recv()
            if phase < steps:
                gather_scale(phase).start()

    acc_g[...] = jnp.zeros_like(acc_g)
    acc_u[...] = jnp.zeros_like(acc_u)

    def up(p, carry):
        columns = pl.ds(pl.multiple_of(p * CHUNK, CHUNK), CHUNK)
        x = x3[:, :, columns].astype(jnp.float32).reshape(rows, CHUNK).astype(jnp.bfloat16)
        x2[...] = x
        for j, acc in enumerate((acc_g, acc_u)):
            slot = lax.rem(2 * p + j, RING)
            arrived(slot)
            for n in range(0, hidden, 256):
                acc[:, n : n + 256] += jnp.dot(
                    x2[...], ring[slot, :, n : n + 256], preferred_element_type=jnp.float32
                )
        q = p + RING // 2

        @pl.when(q < k_count)
        def _():
            load_pair(q)

        for j in range(2):
            d = 2 * (q - k_count) + j

            @pl.when((d >= 0) & (d < k_count))
            def _():
                load_down(d)

        return carry

    lax.fori_loop(0, k_count, up, 0)

    wide = lax.broadcasted_iota(jnp.int32, (rows, 128), 1)
    scale = jnp.sum(
        jnp.where(wide == me // slices, s3[...].reshape(rows, 128), 0.0), axis=1, keepdims=True
    )
    for n in range(0, hidden, 256):
        g = acc_g[:, n : n + 256]
        hid[:, n : n + 256] = (
            g / (1.0 + jnp.exp(-g)) * acc_u[:, n : n + 256] * scale
        ).astype(jnp.bfloat16)

    def reduce(level, c):
        return pltpu.make_async_remote_copy(
            src_ref=snd[level].at[c],
            dst_ref=rcv[level].at[c],
            send_sem=rs_send.at[level, c],
            recv_sem=rs_recv.at[level, c],
            device_id=partner(steps - 1 - level),
            device_id_type=pl.DeviceIdType.MESH,
        )

    def pass_on(level, c, total):
        half = total.shape[0] // 2
        keep[level][c] = total[:half]
        sent = total[half:]
        if half == block:
            sent = jnp.concatenate([sent[:, : CHUNK // 2], sent[:, CHUNK // 2 :]], axis=0)
        snd[level][c] = sent.astype(jnp.bfloat16)
        reduce(level, c).start()

    def down(c, carry):
        for level in range(steps, 0, -1):
            d = c - LAG * level

            @pl.when((d >= 0) & (d < k_count))
            def _():
                reduce(level - 1, d).wait_recv()
                got = rcv[level - 1][d].astype(jnp.float32)
                if level == steps:
                    got = jnp.concatenate([got[:block], got[block:]], axis=1)
                total = keep[level - 1][d] + got
                if level < steps:
                    pass_on(level, d, total)
                else:
                    out[:, pl.ds(pl.multiple_of(d * CHUNK, CHUNK), CHUNK)] = total

        @pl.when(c < k_count)
        def _():
            slot = lax.rem(2 * k_count + c, RING)
            arrived(slot)
            total = jnp.zeros((rows, CHUNK), jnp.float32)
            for k in range(0, hidden, CHUNK):
                total += jnp.dot(
                    hid[:, k : k + CHUNK],
                    ring[slot, :, k : k + CHUNK],
                    preferred_element_type=jnp.float32,
                )
            pass_on(0, c, total)

        return carry

    lax.fori_loop(0, k_count + LAG * steps, down, 0)

    for step in range(steps):
        for a in range(PARTS):
            gather(step, a).wait_send()
        gather_scale(step).wait_send()

    def finish(c, carry):
        for level in range(steps):
            reduce(level, c).wait_send()
        return carry

    lax.fori_loop(0, k_count, finish, 0)


def by_kernel(bits, tokens, routes, gate_scale, w_gate, w_up, w_down):
    steps = len(bits)
    block, width = tokens.shape
    hidden = w_gate.shape[2]
    rows = block << steps
    count = width // CHUNK
    halves = [rows >> (level + 1) for level in range(steps)]
    sent = [(count, h, CHUNK) if h > block else (count, 2 * h, CHUNK // 2) for h in halves]
    vmem = pl.BlockSpec(memory_space=pltpu.VMEM)
    hbm = pl.BlockSpec(memory_space=pl.ANY)
    result = pl.pallas_call(
        functools.partial(kernel, bits, FF // hidden),
        out_shape=jax.ShapeDtypeStruct((block, width), jnp.float32),
        in_specs=[vmem, vmem, vmem, hbm, hbm, hbm],
        out_specs=vmem,
        scratch_shapes=[
            pltpu.VMEM((1 << steps, block, width), jnp.bfloat16),
            pltpu.VMEM((rows, CHUNK), jnp.bfloat16),
            pltpu.VMEM((1 << steps, block, 128), jnp.float32),
            pltpu.VMEM((rows, hidden), jnp.float32),
            pltpu.VMEM((rows, hidden), jnp.float32),
            pltpu.VMEM((rows, hidden), jnp.bfloat16),
            pltpu.VMEM((RING, CHUNK, hidden), jnp.bfloat16),
            [pltpu.VMEM((count, h, CHUNK), jnp.float32) for h in halves],
            [pltpu.VMEM(s, jnp.bfloat16) for s in sent],
            [pltpu.VMEM(s, jnp.bfloat16) for s in sent],
            pltpu.SemaphoreType.DMA((RING,)),
            pltpu.SemaphoreType.DMA((steps, PARTS)),
            pltpu.SemaphoreType.DMA((steps, PARTS)),
            pltpu.SemaphoreType.DMA((steps,)),
            pltpu.SemaphoreType.DMA((steps,)),
            pltpu.SemaphoreType.DMA((steps, count)),
            pltpu.SemaphoreType.DMA((steps, count)),
        ],
        compiler_params=pltpu.CompilerParams(
            collective_id=0, has_side_effects=True, vmem_limit_bytes=VMEM
        ),
    )(tokens, routes, gate_scale, w_gate, w_up, w_down)
    return result.astype(jnp.bfloat16)


def solution(mesh):
    devices = mesh.shape["expert"]

    def on_device(tokens, routes, gate_scale, w_gate, w_up, w_down):
        if devices == 16 and w_gate.shape[2] == FF:
            return by_kernel(
                (2, 3, 1, 0), tokens, routes, gate_scale, w_gate, w_up, w_down
            )
        return by_all_to_all(tokens, routes, gate_scale, w_gate, w_up, w_down)

    return jax.shard_map(
        on_device,
        mesh=mesh,
        in_specs=(
            P(("groups", "expert"), None),
            P(("groups", "expert"), None),
            P(("groups", "expert"), None),
            P("expert", None, None),
            P("expert", None, None),
            P("expert", None, None),
        ),
        out_specs=P(("groups", "expert"), None),
        check_vma=False,
    )
```

```python
import functools
import math

import jax
import jax.numpy as jnp
from jax import lax
from jax.experimental import pallas as pl
from jax.experimental.pallas import tpu as pltpu
from jax.sharding import PartitionSpec as P

FF = 2048
CHUNK = 512
RING = 22
PARTS = 7
LAG = 6
VMEM = 62 * 2**20


def by_all_to_all(tokens, routes, gate_scale, w_gate, w_up, w_down):
    devices = lax.axis_size("expert")
    tok_count, top_count = routes.shape
    width = tokens.shape[1]
    slices = FF // w_gate.shape[2]
    experts = devices // slices
    capacity = tok_count * top_count // experts + 2
    flat = routes.reshape(-1)
    onehot = (flat[:, None] == jnp.arange(experts, dtype=jnp.int32)[None, :]).astype(jnp.int32)
    slot = jnp.sum((jnp.cumsum(onehot, axis=0) - onehot) * onehot, axis=1)
    position = flat * capacity + slot
    picks = position[:, None] == jnp.arange(experts * capacity, dtype=jnp.int32)[None, :]
    picks = picks.reshape(tok_count, top_count, experts * capacity)
    select = jnp.any(picks, axis=1).astype(jnp.bfloat16)
    buffer = lax.dot_general(
        select, tokens, (((0,), (0,)), ((), ())), preferred_element_type=jnp.float32
    ).astype(jnp.bfloat16)
    outgoing = jnp.broadcast_to(
        buffer.reshape(experts, 1, capacity, width), (experts, slices, capacity, width)
    )
    outgoing = outgoing.reshape(devices, capacity, width)
    arrived = lax.all_to_all(outgoing, "expert", split_axis=0, concat_axis=0, tiled=True)
    count = arrived.shape[1]
    flat_rows = arrived.reshape(-1, width)
    gate = jnp.dot(flat_rows, w_gate[0], preferred_element_type=jnp.float32)
    upper = jnp.dot(flat_rows, w_up[0], preferred_element_type=jnp.float32)
    hidden = (jax.nn.silu(gate) * upper).astype(jnp.bfloat16)
    result = jnp.dot(hidden, w_down[0], preferred_element_type=jnp.float32).astype(jnp.bfloat16)
    back = lax.all_to_all(
        result.reshape(devices, count, width), "expert", split_axis=0, concat_axis=0, tiled=True
    )
    summed = back.reshape(experts, slices, capacity, width).astype(jnp.float32).sum(axis=1)
    summed = summed.reshape(experts * capacity, width)
    weights = jnp.sum(picks.astype(jnp.float32) * gate_scale[:, :, None], axis=1)
    mixed = jnp.dot(
        weights, summed, precision=lax.Precision.HIGHEST, preferred_element_type=jnp.float32
    )
    return mixed.astype(jnp.bfloat16)


EXCHANGES = ((1, 1), (2, 1), (3, 1), (4, 4), (8, 8))


def kernel(
    bits, slices, tok, routes, gates, wg, wu, wd, out,
    x3, x2, s3, acc_g, acc_u, hid, ring, keep, snd, rcv,
    ring_sem, ag_send, ag_recv, sc_send, sc_recv, rs_send, rs_recv,
):
    block, width = tok.shape
    rows = 16 * block
    hidden = wg.shape[2]
    k_count = width // CHUNK
    part = width // PARTS
    per_part = part // CHUNK
    me = lax.axis_index("expert")

    def partner(moves):
        there = me
        for j, place in enumerate(bits):
            if (moves >> j) & 1:
                there = there + (1 - 2 * ((me // place) % 2)) * place
        return {"expert": there}

    def load_pair(p):
        for j, w in enumerate((wg, wu)):
            slot = lax.rem(2 * p + j, RING)
            pltpu.make_async_copy(
                w.at[0, pl.ds(p * CHUNK, CHUNK), :], ring.at[slot], ring_sem.at[slot]
            ).start()

    def load_down(d):
        slot = lax.rem(2 * k_count + d, RING)
        for k in range(hidden // CHUNK):
            pltpu.make_async_copy(
                wd.at[0, pl.ds(k * CHUNK, CHUNK), pl.ds(d * CHUNK, CHUNK)],
                ring.at[slot, :, pl.ds(k * CHUNK, CHUNK)],
                ring_sem.at[slot],
            ).start()

    def arrived(slot):
        pltpu.make_async_copy(ring.at[slot], ring.at[slot], ring_sem.at[slot]).wait()

    def first(p, carry):
        load_pair(p)
        return carry

    lax.fori_loop(0, RING // 2, first, 0)

    barrier = pltpu.get_barrier_semaphore()
    for moves in (1, 2, 3, 4, 8):
        pl.semaphore_signal(
            barrier, inc=1, device_id=partner(moves), device_id_type=pl.DeviceIdType.MESH
        )
    x3[0] = tok[...]
    lane = lax.broadcasted_iota(jnp.int32, (block, 128), 1)
    dense = jnp.zeros((block, 128), jnp.float32)
    for k in range(routes.shape[1]):
        dense += jnp.where(routes[:, k : k + 1] == lane, gates[:, k : k + 1], 0.0)
    s3[0] = dense
    pl.semaphore_wait(barrier, 5)

    def gather(lane_of, a):
        moves, held = EXCHANGES[lane_of]
        columns = pl.ds(pl.multiple_of(a * part, part), part)
        return pltpu.make_async_remote_copy(
            src_ref=x3.at[pl.ds(0, held), :, columns],
            dst_ref=x3.at[pl.ds(moves, held), :, columns],
            send_sem=ag_send.at[lane_of, a],
            recv_sem=ag_recv.at[lane_of, a],
            device_id=partner(moves),
            device_id_type=pl.DeviceIdType.MESH,
        )

    def gather_scale(lane_of):
        moves, held = EXCHANGES[lane_of]
        return pltpu.make_async_remote_copy(
            src_ref=s3.at[pl.ds(0, held)],
            dst_ref=s3.at[pl.ds(moves, held)],
            send_sem=sc_send.at[lane_of],
            recv_sem=sc_recv.at[lane_of],
            device_id=partner(moves),
            device_id_type=pl.DeviceIdType.MESH,
        )

    def open_part(a, carry):
        for lane_of in range(3):
            gather(lane_of, a).start()
        return carry

    lax.fori_loop(0, PARTS, open_part, 0)
    for lane_of in range(3):
        gather_scale(lane_of).start()

    acc_g[...] = jnp.zeros_like(acc_g)
    acc_u[...] = jnp.zeros_like(acc_u)

    def up(p, carry):
        columns = pl.ds(pl.multiple_of(p * CHUNK, CHUNK), CHUNK)
        x = x3[:, :, columns].astype(jnp.float32).reshape(rows, CHUNK).astype(jnp.bfloat16)
        x2[...] = x
        for j, acc in enumerate((acc_g, acc_u)):
            slot = lax.rem(2 * p + j, RING)
            arrived(slot)
            for n in range(0, hidden, 256):
                acc[:, n : n + 256] += jnp.dot(
                    x2[...], ring[slot, :, n : n + 256], preferred_element_type=jnp.float32
                )
        q = p + RING // 2

        @pl.when(q < k_count)
        def _():
            load_pair(q)

        for j in range(2):
            d = 2 * (q - k_count) + j

            @pl.when((d >= 0) & (d < k_count))
            def _():
                load_down(d)

        return carry

    def phase_of(phase, carry):
        @pl.when(phase < PARTS)
        def _():
            for lane_of in range(3):
                gather(lane_of, phase).wait_recv()
            gather(3, phase).start()

        @pl.when((phase >= 1) & (phase <= PARTS))
        def _():
            gather(3, phase - 1).wait_recv()
            gather(4, phase - 1).start()

        @pl.when(phase == 0)
        def _():
            for lane_of in range(3):
                gather_scale(lane_of).wait_recv()
            gather_scale(3).start()

        @pl.when(phase == 1)
        def _():
            gather_scale(3).wait_recv()
            gather_scale(4).start()

        @pl.when(phase >= 2)
        def _():
            gather(4, phase - 2).wait_recv()
            lax.fori_loop((phase - 2) * per_part, (phase - 1) * per_part, up, 0)

        return carry

    lax.fori_loop(0, PARTS + 2, phase_of, 0)
    gather_scale(4).wait_recv()

    wide = lax.broadcasted_iota(jnp.int32, (rows, 128), 1)
    scale = jnp.sum(
        jnp.where(wide == me // slices, s3[...].reshape(rows, 128), 0.0), axis=1, keepdims=True
    )
    for n in range(0, hidden, 256):
        g = acc_g[:, n : n + 256]
        hid[:, n : n + 256] = (
            g / (1.0 + jnp.exp(-g)) * acc_u[:, n : n + 256] * scale
        ).astype(jnp.bfloat16)

    def reduce(level, c):
        moves = (8, 4)[level]
        return pltpu.make_async_remote_copy(
            src_ref=snd[level].at[c],
            dst_ref=rcv[level].at[c],
            send_sem=rs_send.at[level, c],
            recv_sem=rs_recv.at[level, c],
            device_id=partner(moves),
            device_id_type=pl.DeviceIdType.MESH,
        )

    def reduce_last(moves, c):
        return pltpu.make_async_remote_copy(
            src_ref=snd[2].at[c, moves - 1],
            dst_ref=rcv[2].at[c, moves - 1],
            send_sem=rs_send.at[1 + moves, c],
            recv_sem=rs_recv.at[1 + moves, c],
            device_id=partner(moves),
            device_id_type=pl.DeviceIdType.MESH,
        )

    def pass_on(level, c, total):
        if level < 2:
            half = total.shape[0] // 2
            keep[level][c] = total[:half]
            snd[level][c] = total[half:].astype(jnp.bfloat16)
            reduce(level, c).start()
            return
        keep[2][c] = total[:block]
        for moves in (1, 2, 3):
            sent = total[moves * block : (moves + 1) * block]
            sent = jnp.concatenate([sent[:, : CHUNK // 2], sent[:, CHUNK // 2 :]], axis=0)
            snd[2][c, moves - 1] = sent.astype(jnp.bfloat16)
            reduce_last(moves, c).start()

    def down(c, carry):
        for level in (3, 2, 1):
            d = c - LAG * level

            @pl.when((d >= 0) & (d < k_count))
            def _():
                total = keep[level - 1][d]
                if level < 3:
                    reduce(level - 1, d).wait_recv()
                    pass_on(level, d, total + rcv[level - 1][d].astype(jnp.float32))
                else:
                    for moves in (1, 2, 3):
                        reduce_last(moves, d).wait_recv()
                        got = rcv[2][d, moves - 1].astype(jnp.float32)
                        total += jnp.concatenate([got[:block], got[block:]], axis=1)
                    out[:, pl.ds(pl.multiple_of(d * CHUNK, CHUNK), CHUNK)] = total

        @pl.when(c < k_count)
        def _():
            slot = lax.rem(2 * k_count + c, RING)
            arrived(slot)
            total = jnp.zeros((rows, CHUNK), jnp.float32)
            for k in range(0, hidden, CHUNK):
                total += jnp.dot(
                    hid[:, k : k + CHUNK],
                    ring[slot, :, k : k + CHUNK],
                    preferred_element_type=jnp.float32,
                )
            pass_on(0, c, total)

        return carry

    lax.fori_loop(0, k_count + LAG * 3, down, 0)

    def close_part(a, carry):
        for lane_of in range(5):
            gather(lane_of, a).wait_send()
        return carry

    lax.fori_loop(0, PARTS, close_part, 0)
    for lane_of in range(5):
        gather_scale(lane_of).wait_send()

    def finish(c, carry):
        for level in range(2):
            reduce(level, c).wait_send()
        for moves in (1, 2, 3):
            reduce_last(moves, c).wait_send()
        return carry

    lax.fori_loop(0, k_count, finish, 0)


def by_kernel(bits, tokens, routes, gate_scale, w_gate, w_up, w_down):
    steps = len(bits)
    block, width = tokens.shape
    hidden = w_gate.shape[2]
    rows = block << steps
    count = width // CHUNK
    halves = [rows // 2, rows // 4, block]
    sent = [(count, h, CHUNK) for h in halves[:2]] + [(count, 3, 2 * block, CHUNK // 2)]
    vmem = pl.BlockSpec(memory_space=pltpu.VMEM)
    hbm = pl.BlockSpec(memory_space=pl.ANY)
    result = pl.pallas_call(
        functools.partial(kernel, bits, FF // hidden),
        out_shape=jax.ShapeDtypeStruct((block, width), jnp.float32),
        in_specs=[vmem, vmem, vmem, hbm, hbm, hbm],
        out_specs=vmem,
        scratch_shapes=[
            pltpu.VMEM((1 << steps, block, width), jnp.bfloat16),
            pltpu.VMEM((rows, CHUNK), jnp.bfloat16),
            pltpu.VMEM((1 << steps, block, 128), jnp.float32),
            pltpu.VMEM((rows, hidden), jnp.float32),
            pltpu.VMEM((rows, hidden), jnp.float32),
            pltpu.VMEM((rows, hidden), jnp.bfloat16),
            pltpu.VMEM((RING, CHUNK, hidden), jnp.bfloat16),
            [pltpu.VMEM((count, h, CHUNK), jnp.float32) for h in halves],
            [pltpu.VMEM(s, jnp.bfloat16) for s in sent],
            [pltpu.VMEM(s, jnp.bfloat16) for s in sent],
            pltpu.SemaphoreType.DMA((RING,)),
            pltpu.SemaphoreType.DMA((5, PARTS)),
            pltpu.SemaphoreType.DMA((5, PARTS)),
            pltpu.SemaphoreType.DMA((5,)),
            pltpu.SemaphoreType.DMA((5,)),
            pltpu.SemaphoreType.DMA((5, count)),
            pltpu.SemaphoreType.DMA((5, count)),
        ],
        compiler_params=pltpu.CompilerParams(
            collective_id=0, has_side_effects=True, vmem_limit_bytes=VMEM
        ),
    )(tokens, routes, gate_scale, w_gate, w_up, w_down)
    return result.astype(jnp.bfloat16)


def solution(mesh):
    devices = mesh.shape["expert"]

    def on_device(tokens, routes, gate_scale, w_gate, w_up, w_down):
        if devices == 16 and w_gate.shape[2] == FF:
            return by_kernel(
                (4, 8, 2, 1), tokens, routes, gate_scale, w_gate, w_up, w_down
            )
        return by_all_to_all(tokens, routes, gate_scale, w_gate, w_up, w_down)

    return jax.shard_map(
        on_device,
        mesh=mesh,
        in_specs=(
            P(("groups", "expert"), None),
            P(("groups", "expert"), None),
            P(("groups", "expert"), None),
            P("expert", None, None),
            P("expert", None, None),
            P("expert", None, None),
        ),
        out_specs=P(("groups", "expert"), None),
        check_vma=False,
    )
```
